256 devices in a mesh: dom: 8 (over y, core), dev: 32 (over z, x).
Axes of the slice: x: 4, y: 4, z: 8, core: 2. Of those that a mesh axis runs over, the one named last changes fastest.
Arguments:
- start_block: float32 [589824, 128], P(('dom', 'dev')), may hold values from -8 to 8
- columns: int32 [4608, 4], P(('dom', 'dev')), may hold values from 0 to 4607, as said below
- edge_weights: int32 [4608, 4, 128, 128], P(('dom', 'dev')), may hold values from 0 to 1023, as said below
Outputs:
- filtered: float32 [589824, 128], P(('dom', 'dev'))
- ritz: float32 [128, 128], replicated
The draws below stay inside these ranges and needn't reach their ends.
Inputs may be any that keep to these rules, and one draw needn't show every extreme that they name: `columns`: A device holds 18 consecutive tile-rows, and a part 32 consecutive devices. Each tile-row lists first its own diagonal tile, then a tile of the same device. Over one device's tile-rows, exactly one reference goes to each device of the same part whose index within the part differs from its own by 1 to 4, cyclically, in either direction, and exactly one to the device of the same part whose index differs by 16; 8 references go to the device of the same index within another part, every other part once and one of them twice; all other references are to tiles of the same device. `edge_weights`: each row of a tile-row has its own power of two between 16 and 1024 that bounds its entries; the diagonal entries of the diagonal tile are at least half of that power.
All inputs are finite; a program needn't handle non-finite values.
Results may differ from the reference program's by a relative error of at most 0.0003.
Values sent between devices are 32-bit elements; how exact they have to be, the bound alone decides.
A program may use at most 128 MiB of HBM per device.

```python
import jax
import jax.numpy as jnp
from jax import lax

WIDTH = 128
TILE = 128
TROWS = 18
DEGREE = 5
PASSES = 1
REACH = 4
TILEROWS = 4608
NROWS = 589824
N_DOM = 8
N_DEV = 32


def draw_columns(key, part):
    key = jax.random.fold_in(key, 11)
    keys = jax.random.split(key, 6)
    block_count = N_DOM * N_DEV
    blocks = jnp.arange(block_count, dtype=jnp.int32)
    part_of = (blocks // N_DEV)[:, None]
    device_of = (blocks % N_DEV)[:, None]
    orders = jax.vmap(lambda single: jax.random.permutation(single, TROWS))(jax.random.split(keys[0], block_count))
    position = jnp.argsort(orders, axis=1).astype(jnp.int32)
    rows = jnp.arange(TROWS, dtype=jnp.int32)[None, :]
    base = blocks[:, None] * TROWS
    same_one = base + jax.random.randint(keys[1], (block_count, TROWS), 0, TROWS)
    same_two = base + jax.random.randint(keys[2], (block_count, TROWS), 0, TROWS)
    same_three = base + jax.random.randint(keys[3], (block_count, TROWS), 0, TROWS)
    offset = jnp.where(position < REACH, position + 1, jnp.where(position < 2 * REACH, -(position - REACH + 1), N_DEV // 2))
    peer = (device_of + offset) % N_DEV
    inner = (part_of * N_DEV + peer) * TROWS + jax.random.randint(keys[4], (block_count, TROWS), 0, TROWS)
    outer_position = position - 2 * REACH - 1
    extra = jax.random.randint(keys[5], (block_count, 1), 0, N_DOM - 1)
    part_offset = jnp.where(outer_position < N_DOM - 1, outer_position + 1, 1 + extra)
    target_part = (part_of + part_offset) % N_DOM
    outer = (target_part * N_DEV + device_of) * TROWS + jax.random.randint(jax.random.fold_in(keys[4], 5), (block_count, TROWS), 0, TROWS)
    third = jnp.where(position < 2 * REACH + 1, inner, same_two)
    fourth = jnp.where((position >= 2 * REACH + 1) & (position < 2 * REACH + 1 + N_DOM), outer, same_three)
    listed = jnp.stack([base + rows, same_one, third, fourth], axis=-1)
    return listed.reshape(TILEROWS, 4).astype(jnp.int32)


def draw_edge_weights(key, part):
    key = jax.random.fold_in(key, 23)
    key_power, key_raw = jax.random.split(key, 2)
    exponent = jax.random.randint(key_power, (TILEROWS, 1, TILE, 1), 4, 11)
    bound_power = jnp.left_shift(jnp.int32(1), exponent)
    raw = jax.random.randint(key_raw, (TILEROWS, 4, TILE, TILE), 0, 4096)
    keep = raw % 4 == 0
    value = jnp.where(keep, raw // 4 % bound_power, 0)
    half = bound_power // 2
    diagonal = half + raw // 4 % half
    row_ids = jnp.arange(TILE)[None, None, :, None]
    col_ids = jnp.arange(TILE)[None, None, None, :]
    slot_ids = jnp.arange(4)[None, :, None, None]
    on_diagonal = (row_ids == col_ids) & (slot_ids == 0)
    return jnp.where(on_diagonal, diagonal, value).astype(jnp.int32)


def draw_start_block(key, part):
    key = jax.random.fold_in(key, 37)
    key_base = jax.random.fold_in(key, 0)
    values = jax.random.normal(key_base, (NROWS, WIDTH), jnp.float32)
    return jnp.clip(values, -8.0, 8.0).astype(jnp.float32)


def setup_inputs(seed: int = 0) -> dict:
    key_of = jax.random.split(jax.random.key(seed), 4)
    start_block = draw_start_block(jax.random.fold_in(key_of[3], 71), 0)
    columns = draw_columns(jax.random.fold_in(key_of[3], 71), 0)
    edge_weights = draw_edge_weights(jax.random.fold_in(key_of[3], 71), 0)
    return dict(start_block=start_block, columns=columns, edge_weights=edge_weights)


epsilon = 1e-06
center = 1.025
half_width = 0.975

def reference(start_block, columns, edge_weights):
    block_count = N_DOM * N_DEV
    weight_blocks = edge_weights.reshape(block_count, TROWS, 4, TILE, TILE)
    degree = lax.map(lambda weight_piece: lax.optimization_barrier(jnp.sum(weight_piece.astype(jnp.float32), axis=(1, 3))), weight_blocks)
    degree = degree.reshape(TILEROWS, TILE)
    row_scale = lax.rsqrt(degree)
    column_blocks = columns.reshape(block_count, TROWS, 4)
    scale_blocks = row_scale.reshape(block_count, TROWS, TILE)

    def apply_laplacian(field):
        scaled = row_scale[:, :, None] * field

        def one_block(pieces):
            weight_piece, column_piece, field_piece, scale_piece = pieces
            operand = scaled[column_piece]
            product = jnp.einsum('rkij,rkjw->riw', weight_piece.astype(jnp.float32), operand, precision=lax.Precision.HIGHEST)
            return field_piece - scale_piece[:, :, None] * product
        result = lax.map(one_block, (weight_blocks, column_blocks, field.reshape(block_count, TROWS, TILE, WIDTH), scale_blocks))
        return result.reshape(TILEROWS, TILE, WIDTH)
    field = start_block.reshape(TILEROWS, TILE, WIDTH)
    for pass_number in range(PASSES):
        totals = lax.optimization_barrier(jnp.sum(field * field, axis=(0, 1)))
        factor = lax.rsqrt(totals / NROWS + epsilon)
        first = field * factor
        older = first
        newer = (apply_laplacian(first) - center * first) / half_width
        for degree_step in range(2, DEGREE + 1):
            older, newer = (newer, 2.0 * (apply_laplacian(newer) - center * newer) / half_width - older)
        field = newer
    image = apply_laplacian(field)
    flat = field.reshape(NROWS, WIDTH)
    gram = jnp.dot(flat.T.astype(jnp.float32), flat.astype(jnp.float32), precision=lax.Precision.HIGHEST, preferred_element_type=jnp.float32) / NROWS
    projected = jnp.dot(flat.T.astype(jnp.float32), image.reshape(NROWS, WIDTH).astype(jnp.float32), precision=lax.Precision.HIGHEST, preferred_element_type=jnp.float32) / NROWS
    lower = jnp.linalg.cholesky(gram)
    left_solved = jax.scipy.linalg.solve_triangular(lower, projected, lower=True)
    ritz = jax.scipy.linalg.solve_triangular(lower, left_solved.T, lower=True).T
    return (flat, ritz)
```

```python
import functools

import jax
import jax.numpy as jnp
from jax import lax
from jax.experimental import pallas as pl
from jax.experimental.pallas import tpu as pltpu
from jax.sharding import PartitionSpec as P

TILE = 128
WIDTH = 128
TROWS = 18
DEGREE = 5
N_DOM = 8
N_DEV = 32
NROWS = 589824
HALF = 64
INNER = (1, 2, 3, 4, -1, -2, -3, -4, 16)
OUTER = ((0, 1), (1, 0), (1, 1), (2, 0), (2, 1), (3, 0), (3, 1))
N_IN = 9
N_OUT = 7
N_MSG = N_IN + N_OUT
N_SLOT = N_MSG + 4
N_SRC = TROWS + N_SLOT

epsilon = 1e-06
center = 1.025
half_width = 0.975

MESH = pl.DeviceIdType.MESH
NT = (((1,), (1,)), ((), ()))


def tables(columns):
    dom = lax.axis_index("dom")
    dev = lax.axis_index("dev")
    flat = columns.reshape(-1)
    owner = flat // TROWS
    tile = flat % TROWS
    part = owner // N_DEV
    is_local = owner == dom * N_DEV + dev
    is_outer = part != dom
    is_inner = jnp.logical_not(is_local | is_outer)
    off = (owner % N_DEV - dev) % N_DEV
    inner_slot = jnp.where(off <= 4, off - 1, jnp.where(off == 16, 8, 35 - off))
    dy = (part // 2 - dom // 2) % 4
    dc = (part + dom) % 2
    outer_slot = 2 * dy + dc - 1
    ids = jnp.arange(flat.shape[0], dtype=jnp.int32)
    same = is_outer[None, :] & is_outer[:, None] & (part[None, :] == part[:, None]) & (ids[None, :] < ids[:, None])
    is_extra = jnp.any(same, axis=1)
    source = jnp.where(
        is_local,
        tile,
        jnp.where(
            is_inner,
            TROWS + inner_slot,
            jnp.where(is_extra, TROWS + N_MSG + dy, TROWS + N_IN + outer_slot),
        ),
    )
    slot = jnp.where(is_inner, inner_slot, jnp.where(is_outer & jnp.logical_not(is_extra), N_IN + outer_slot, -1))
    msg_ids = jnp.arange(N_MSG, dtype=jnp.int32)[:, None]
    base = jnp.sum(jnp.where(slot[None, :] == msg_ids, tile[None, :], 0), axis=1)
    out_ids = msg_ids - N_IN
    relayed = (out_ids > 0) & (out_ids % 2 == 1) & (outer_slot[None, :] == out_ids + 1)
    extra = jnp.where(
        is_extra[None, :],
        jnp.where(
            outer_slot[None, :] == out_ids,
            tile[None, :],
            jnp.where(relayed, TROWS + (out_ids + 1) // 2 - 1, 0),
        ),
        0,
    )
    extra = jnp.sum(extra, axis=1)
    lanes = jnp.arange(128, dtype=jnp.int32)[None, :]
    msg = jnp.where(lanes == 0, base[:, None], jnp.where(lanes == 1, extra[:, None], 0))
    return source.astype(jnp.int32), msg.astype(jnp.int32)[:, None, :]


def split(x):
    hi = x.astype(jnp.bfloat16)
    mid = (x - hi.astype(jnp.float32)).astype(jnp.bfloat16)
    return hi, mid


def quad(x):
    n = x.shape[0] // 2
    return (x[n:, 128:] + x[n:, :128]) + (x[:n, 128:] + x[:n, :128])


def kernel(
    source, msg, start, weights,
    filtered, ritz,
    wb, scale, y, zf, zb, part, mul, stage, recv, relay,
    got, serve, fb, ib, sq, sqs, sqd, sqx, sqz, red, r1, r2, r3, rg, mat_a, mat_m,
    msg_ss, msg_rs, smem_sem, ss, rs, relay_ss, relay_rs,
    sq_ss, sq_rs, g_ss, g_rs,
):
    dom = lax.axis_index("dom")
    dev = lax.axis_index("dev")
    yy, core = dom // 2, dom % 2
    zz, xx = dev // 4, dev % 4

    def inner_peer(offset):
        return (dom, (dev + offset + N_DEV) % N_DEV)

    def outer_peer(dy, dc):
        return (((yy + dy) % 4) * 2 + (core + dc) % 2, dev)

    def x_peer(d):
        return (dom, zz * 4 + (xx + d) % 4)

    def z_peer(d):
        return (dom, ((zz + d) % 8) * 4 + xx)

    def requester(s):
        if s < N_IN:
            return inner_peer(-INNER[s])
        dy, dc = OUTER[s - N_IN]
        return outer_peer(4 - dy, dc)

    barrier = pltpu.get_barrier_semaphore()
    peers = [inner_peer(o) for o in INNER] + [outer_peer(*o) for o in OUTER]
    peers += [z_peer(d) for d in (2, 3, 5, 6)]
    for peer in peers:
        pl.semaphore_signal(barrier, inc=1, device_id=peer, device_id_type=MESH)

    def turn(r, total):
        tile = start[r].T
        y[0, 0, r] = tile[:HALF]
        y[0, 1, r] = tile[HALF:]
        y[1, 0, r] = jnp.zeros((HALF, TILE), jnp.float32)
        y[1, 1, r] = jnp.zeros((HALF, TILE), jnp.float32)
        return total + tile * tile

    squares = lax.fori_loop(0, TROWS, turn, jnp.zeros((WIDTH, TILE), jnp.float32))
    mul[...] = jnp.ones_like(mul)
    sq[...] = lax.dot_general(
        jnp.ones((8, TILE), jnp.float32), squares, NT,
        precision=lax.Precision.HIGHEST, preferred_element_type=jnp.float32,
    )

    pl.semaphore_wait(barrier, len(peers))

    def msg_copy(s):
        return pltpu.make_async_remote_copy(
            src_ref=msg.at[s], dst_ref=got.at[s], send_sem=msg_ss.at[s], recv_sem=msg_rs.at[s],
            device_id=inner_peer(INNER[s]) if s < N_IN else outer_peer(*OUTER[s - N_IN]),
            device_id_type=MESH,
        )

    for s in range(N_MSG):
        msg_copy(s).start()

    def dom_copy(src, dst, o, send, recv_sem):
        dy, dc = OUTER[o]
        return pltpu.make_async_remote_copy(
            src_ref=src, dst_ref=dst, send_sem=send, recv_sem=recv_sem,
            device_id=outer_peer(dy, dc), device_id_type=MESH,
        )

    def sq_dom(o):
        return dom_copy(sq, sqd.at[o], o, sq_ss.at[o], sq_rs.at[o])

    def sq_x(d):
        return pltpu.make_async_remote_copy(
            src_ref=sqs.at[0], dst_ref=sqx.at[d - 1], send_sem=sq_ss.at[6 + d], recv_sem=sq_rs.at[6 + d],
            device_id=x_peer(d), device_id_type=MESH,
        )

    def sq_z(d):
        return pltpu.make_async_remote_copy(
            src_ref=sqs.at[1], dst_ref=sqz.at[d - 1], send_sem=sq_ss.at[9 + d], recv_sem=sq_rs.at[9 + d],
            device_id=z_peer(d), device_id_type=MESH,
        )

    for o in range(N_OUT):
        sq_dom(o).start()

    ones = jnp.ones((8, 256), jnp.bfloat16)

    def prepare(r, _):
        degree = jnp.zeros((8, 256), jnp.float32)
        for k in range(4):
            w = weights[r, k].astype(jnp.float32)
            hi, lo = split(w)
            cols = pl.ds((k % 2) * 128, 128)
            wb[r, k // 2, pl.ds(0, 128), cols] = hi
            wb[r, k // 2, pl.ds(128, 128), cols] = lo
        for p in range(2):
            degree += lax.dot_general(ones, wb[r, p], NT, preferred_element_type=jnp.float32)
        scale[r] = lax.rsqrt(degree[:, :128] + degree[:, 128:])
        return 0

    lax.fori_loop(0, TROWS, prepare, 0)

    for s in range(N_MSG):
        msg_copy(s).wait()
    to_smem = pltpu.make_async_copy(got, serve, smem_sem)
    to_smem.start()
    to_smem.wait()

    def put_scaled(h, r, value):
        z = value * scale[r, pl.ds(0, 1), :]
        zf[h, r] = z
        hi, mid = split(z)
        zb[h, r, pl.ds(0, HALF), :] = hi
        zb[h, r, pl.ds(HALF, HALF), :] = mid

    def slot_copy(h, par, s):
        if s < N_MSG:
            to = requester(s)
        elif s == N_MSG:
            to = outer_peer(0, 1)
        else:
            to = outer_peer(4 - (s - N_MSG), 0)
        return pltpu.make_async_remote_copy(
            src_ref=stage.at[h, s], dst_ref=recv.at[h, par, s],
            send_sem=ss.at[h, s], recv_sem=rs.at[h, par, s],
            device_id=to, device_id_type=MESH,
        )

    def relay_copy(h, par, d):
        return pltpu.make_async_remote_copy(
            src_ref=stage.at[h, N_SLOT + d], dst_ref=relay.at[h, par, d],
            send_sem=relay_ss.at[h, d], recv_sem=relay_rs.at[h, par, d],
            device_id=outer_peer(0, 1), device_id_type=MESH,
        )

    def send_first(h, par):
        for d in range(3):
            stage[h, N_SLOT + d] = zf[h, serve[N_IN + 2 * (d + 1), 0, 1]]
            relay_copy(h, par, d).start()
        for s in (9, 10, 11, 12, 13, 14, 15, 8, 7, 3, 6, 2, 5, 1, 4, 0, 16):
            index = serve[N_IN, 0, 1] if s == N_MSG else serve[s, 0, 0]
            stage[h, s] = zf[h, index]
            slot_copy(h, par, s).start()

    def send_last(h, par):
        for d in range(3):
            relay_copy(h, par, d).wait_recv()
            zf[h, TROWS + d] = relay[h, par, d]
        for d in range(3):
            s = N_MSG + 1 + d
            stage[h, s] = zf[h, serve[N_IN + 2 * (d + 1) - 1, 0, 1]]
            slot_copy(h, par, s).start()

    def operand(h, r, k):
        return jnp.concatenate([zb[h, source[4 * r + k]], zb[h, source[4 * r + k + 1]]], axis=1)

    def near(h):
        def one(r, _):
            part[h, r] = quad(lax.dot_general(operand(h, r, 0), wb[r, 0], NT, preferred_element_type=jnp.float32))
            return 0
        lax.fori_loop(0, TROWS, one, 0, unroll=6)

    for h in range(2):
        def first(r, _):
            put_scaled(h, r, y[0, h, r])
            return 0
        lax.fori_loop(0, TROWS, first, 0)
        send_first(h, 0)
    for h in range(2):
        near(h)
        send_last(h, 0)

    def iteration(it, _):
        s, h = it // 2, it % 2
        par = s % 2

        @pl.when(it == 2)
        def _():
            for o in range(N_OUT):
                sq_dom(o).wait()
            total = sq[...]
            for o in range(N_OUT):
                total += sqd[o]
            sqs[0] = total
            for d in range(1, 4):
                sq_x(d).start()

        @pl.when(it == 4)
        def _():
            for d in range(1, 4):
                sq_x(d).wait()
            sqs[1] = (sqs[0] + sqx[0]) + (sqx[1] + sqx[2])
            for d in range(1, 8):
                sq_z(d).start()

        @pl.when(it == 8)
        def _():
            for d in range(1, 8):
                sq_z(d).wait()
            total = sqs[1]
            for d in range(7):
                total += sqz[d]
            factor = lax.rsqrt(total[:1] / NROWS + epsilon)
            factor = jnp.broadcast_to(factor, (WIDTH, WIDTH)).T
            mul[0] = factor[:HALF]
            mul[1] = factor[HALF:]

        @pl.when(it == 10)
        def _():
            mul[...] = jnp.ones_like(mul)

        for q in range(N_SLOT):
            slot_copy(h, par, q).wait_recv()

        def widen(q, _):
            hi, mid = split(recv[h, par, q])
            zb[h, TROWS + q, pl.ds(0, HALF), :] = hi
            zb[h, TROWS + q, pl.ds(HALF, HALF), :] = mid
            return 0
        lax.fori_loop(0, N_SLOT, widen, 0, unroll=4)

        def far(r, _):
            part[h, r] += quad(lax.dot_general(operand(h, r, 2), wb[r, 1], NT, preferred_element_type=jnp.float32))
            return 0
        lax.fori_loop(0, TROWS, far, 0, unroll=6)

        last = s == DEGREE
        a = jnp.where(s == 0, (1 - center) / half_width, jnp.where(last, 1.0, 2 * (1 - center) / half_width)).astype(jnp.float32)
        b = jnp.where(s == 0, -1 / half_width, jnp.where(last, -1.0, -2 / half_width)).astype(jnp.float32)
        c = jnp.where((s == 0) | last, 0.0, -1.0).astype(jnp.float32)

        def update(r, _):
            value = a * y[par, h, r] + b * (part[h, r] * scale[r, pl.ds(0, 1), :]) + c * y[1 - par, h, r]
            value = value * mul[h]
            y[1 - par, h, r] = value
            put_scaled(h, r, value)
            return 0
        lax.fori_loop(0, TROWS, update, 0, unroll=3)

        for q in range(N_SLOT):
            slot_copy(h, par, q).wait_send()
        for d in range(3):
            relay_copy(h, par, d).wait_send()

        @pl.when(s < DEGREE)
        def _():
            send_first(h, 1 - par)
            near(h)
            send_last(h, 1 - par)
        return 0

    lax.fori_loop(0, 2 * (DEGREE + 1), iteration, 0)

    def finish(r, _):
        value = jnp.concatenate([y[1, 0, r], y[1, 1, r]], axis=0)
        filtered[r] = value.T
        hi, mid = split(value)
        fb[r, pl.ds(0, 128), :] = hi
        fb[r, pl.ds(128, 128), :] = mid
        hi, mid = split(jnp.concatenate([y[0, 0, r], y[0, 1, r]], axis=0))
        ib[r, pl.ds(0, 128), :] = hi
        ib[r, pl.ds(128, 128), :] = mid
        return 0
    lax.fori_loop(0, TROWS, finish, 0)

    def gram(r, carry):
        left = fb[r]
        return (
            carry[0] + lax.dot_general(left, left, NT, preferred_element_type=jnp.float32),
            carry[1] + lax.dot_general(left, ib[r], NT, preferred_element_type=jnp.float32),
        )
    zero = jnp.zeros((256, 256), jnp.float32)
    sums = lax.fori_loop(0, TROWS, gram, (zero, zero))
    for i in range(2):
        block = quad(sums[i])
        for d in range(N_DOM):
            red[d, pl.ds(16 * i, 16), :] = block[16 * d:16 * d + 16]

    def g1(o):
        dy, dc = OUTER[o]
        peer_dom = ((yy + dy) % 4) * 2 + (core + dc) % 2
        return dom_copy(red.at[peer_dom], r1.at[o], o, g_ss.at[o], g_rs.at[o])

    for o in range(N_OUT):
        g1(o).start()
    for o in range(N_OUT):
        g1(o).wait()
    total = red[dom]
    for o in range(N_OUT):
        total += r1[o]
    r2[xx] = total

    def g2(d, src):
        return pltpu.make_async_remote_copy(
            src_ref=r2.at[xx], dst_ref=r2.at[src], send_sem=g_ss.at[6 + d], recv_sem=g_rs.at[7 + src],
            device_id=x_peer(d), device_id_type=MESH,
        )

    for d in range(1, 4):
        g2(d, xx).start()
    for d in range(1, 4):
        g2(d, xx).wait_send()
        g2(d, (xx + d) % 4).wait_recv()
    r3[zz] = (r2[0] + r2[1]) + (r2[2] + r2[3])

    def g3(d, src):
        return pltpu.make_async_remote_copy(
            src_ref=r3.at[zz], dst_ref=r3.at[src], send_sem=g_ss.at[9 + d], recv_sem=g_rs.at[11 + src],
            device_id=z_peer(d), device_id_type=MESH,
        )

    for d in range(1, 8):
        g3(d, zz).start()
    for d in range(1, 8):
        g3(d, zz).wait_send()
        g3(d, (zz + d) % 8).wait_recv()
    total = r3[0]
    for d in range(1, 8):
        total += r3[d]
    rg[dom] = total * (1.0 / NROWS)

    def g4(o, src):
        dy, dc = OUTER[o]
        return dom_copy(rg.at[dom], rg.at[src], o, g_ss.at[17 + o], g_rs.at[19 + src])

    for o in range(N_OUT):
        g4(o, dom).start()
    for o in range(N_OUT):
        dy, dc = OUTER[o]
        g4(o, dom).wait_send()
        g4(o, ((yy + dy) % 4) * 2 + (core + dc) % 2).wait_recv()

    rows = lax.broadcasted_iota(jnp.int32, (WIDTH, WIDTH), 0)
    cols = lax.broadcasted_iota(jnp.int32, (WIDTH, WIDTH), 1)
    mat_a[...] = jnp.concatenate([rg[d, pl.ds(0, 16), :] for d in range(N_DOM)], axis=0)
    mat_m[...] = jnp.where(rows == cols, 1.0, 0.0)
    projected = jnp.concatenate([rg[d, pl.ds(16, 16), :] for d in range(N_DOM)], axis=0)

    def eliminate(j, _):
        a = mat_a[...]
        row_a = mat_a[pl.ds(j, 1), :]
        row_m = mat_m[pl.ds(j, 1), :]
        column = jnp.sum(jnp.where(cols == j, a, 0.0), axis=1, keepdims=True)
        pivot = jnp.sum(jnp.where(cols[:1] == j, row_a, 0.0), axis=1, keepdims=True)
        multiplier = jnp.where(rows[:, :1] > j, column / pivot, 0.0)
        mat_a[...] = a - multiplier * row_a
        mat_m[...] = mat_m[...] - multiplier * row_m
        return 0
    lax.fori_loop(0, WIDTH, eliminate, 0)
    pivots = jnp.sum(jnp.where(rows == cols, mat_a[...], 0.0), axis=1, keepdims=True)
    inverse = mat_m[...] * lax.rsqrt(pivots)
    left = jnp.dot(inverse, projected, precision=lax.Precision.HIGHEST, preferred_element_type=jnp.float32)
    ritz[...] = lax.dot_general(left, inverse, NT, precision=lax.Precision.HIGHEST, preferred_element_type=jnp.float32)


def body(start_block, columns, edge_weights):
    source, msg = tables(columns)
    f32, bf16 = jnp.float32, jnp.bfloat16
    vmem = pl.BlockSpec(memory_space=pltpu.VMEM)
    dma = pltpu.SemaphoreType.DMA
    filtered, ritz = pl.pallas_call(
        kernel,
        out_shape=(
            jax.ShapeDtypeStruct((TROWS, TILE, WIDTH), f32),
            jax.ShapeDtypeStruct((WIDTH, WIDTH), f32),
        ),
        in_specs=[pl.BlockSpec(memory_space=pltpu.SMEM), vmem, vmem, vmem],
        out_specs=(vmem, vmem),
        scratch_shapes=[
            pltpu.VMEM((TROWS, 2, 256, 256), bf16),
            pltpu.VMEM((TROWS, 8, TILE), f32),
            pltpu.VMEM((2, 2, TROWS, HALF, TILE), f32),
            pltpu.VMEM((2, TROWS + 3, HALF, TILE), f32),
            pltpu.VMEM((2, N_SRC, 2 * HALF, TILE), bf16),
            pltpu.VMEM((2, TROWS, HALF, TILE), f32),
            pltpu.VMEM((2, HALF, TILE), f32),
            pltpu.VMEM((2, N_SLOT + 3, HALF, TILE), f32),
            pltpu.VMEM((2, 2, N_SLOT, HALF, TILE), f32),
            pltpu.VMEM((2, 2, 3, HALF, TILE), f32),
            pltpu.VMEM((N_MSG, 1, 128), jnp.int32),
            pltpu.SMEM((N_MSG, 1, 128), jnp.int32),
            pltpu.VMEM((TROWS, 256, TILE), bf16),
            pltpu.VMEM((TROWS, 256, TILE), bf16),
            pltpu.VMEM((8, 128), f32),
            pltpu.VMEM((2, 8, 128), f32),
            pltpu.VMEM((7, 8, 128), f32),
            pltpu.VMEM((3, 8, 128), f32),
            pltpu.VMEM((7, 8, 128), f32),
            pltpu.VMEM((N_DOM, 32, 128), f32),
            pltpu.VMEM((7, 32, 128), f32),
            pltpu.VMEM((4, 32, 128), f32),
            pltpu.VMEM((8, 32, 128), f32),
            pltpu.VMEM((N_DOM, 32, 128), f32),
            pltpu.VMEM((WIDTH, WIDTH), f32),
            pltpu.VMEM((WIDTH, WIDTH), f32),
            dma((N_MSG,)), dma((N_MSG,)), dma,
            dma((2, N_SLOT)), dma((2, 2, N_SLOT)), dma((2, 3)), dma((2, 2, 3)),
            dma((17,)), dma((17,)), dma((24,)), dma((27,)),
        ],
        compiler_params=pltpu.CompilerParams(
            collective_id=0, has_side_effects=True, vmem_limit_bytes=56 * 2**20
        ),
        cost_estimate=pl.CostEstimate(flops=8_000_000_000, bytes_accessed=8_000_000, transcendentals=0),
    )(source, msg, start_block.reshape(TROWS, TILE, WIDTH), edge_weights)
    return filtered.reshape(TROWS * TILE, WIDTH), ritz


def solution(mesh):
    in_specs = (
        P(("dom", "dev"), None),
        P(("dom", "dev"), None),
        P(("dom", "dev"), None, None, None),
    )
    out_specs = (P(("dom", "dev"), None), P())
    return jax.shard_map(body, mesh=mesh, in_specs=in_specs, out_specs=out_specs, check_vma=False)
```

```python
import functools

import jax
import jax.numpy as jnp
from jax import lax
from jax.experimental import pallas as pl
from jax.experimental.pallas import tpu as pltpu
from jax.sharding import PartitionSpec as P

TILE = 128
WIDTH = 128
TROWS = 18
DEGREE = 5
N_DOM = 8
N_DEV = 32
NROWS = 589824
HALF = 64
INNER = (1, 2, 3, 4, -1, -2, -3, -4, 16)
OUTER = ((0, 1), (1, 0), (1, 1), (2, 0), (2, 1), (3, 0), (3, 1))
N_IN = 9
N_OUT = 7
N_MSG = N_IN + N_OUT
N_SLOT = N_MSG + 4
N_SRC = TROWS + N_SLOT

epsilon = 1e-06
center = 1.025
half_width = 0.975

MESH = pl.DeviceIdType.MESH
NT = (((1,), (1,)), ((), ()))


def split(x):
    hi = x.astype(jnp.bfloat16)
    mid = (x - hi.astype(jnp.float32)).astype(jnp.bfloat16)
    return hi, mid


def quad(x):
    n = x.shape[0] // 2
    return (x[n:, 128:] + x[n:, :128]) + (x[:n, 128:] + x[:n, :128])


def kernel(
    columns, start_hbm, weights_hbm,
    filtered, ritz,
    source, src_v, msg, start, weights, turned,
    wb, scale, y, zf, zb, part, mul, stage, recv, relay,
    got, serve, fb, ib, sq, sqs, sqd, sqx, sqz, red, r1, r2, r3, rg, mat_a, mat_m, lin,
    in_sem, out_sem, msg_ss, msg_rs, smem_sem, ss, rs, relay_ss, relay_rs,
    sq_ss, sq_rs, g_ss, g_rs,
):
    dom = lax.axis_index("dom")
    dev = lax.axis_index("dev")
    yy, core = dom >> 1, dom & 1
    zz, xx = dev >> 2, dev & 3

    inner = {o: (dom, (dev + o) & (N_DEV - 1)) for o in INNER}
    inner.update({-16: inner[16]})
    outer_doms = {
        (dy, dc): (((yy + dy) & 3) << 1) + ((core + dc) & 1) for dy in range(4) for dc in range(2)
    }
    outer = {key: (value, dev) for key, value in outer_doms.items()}
    x_places = {d: (xx + d) & 3 for d in range(1, 4)}
    z_places = {d: (zz + d) & 7 for d in range(1, 8)}
    x_peers = {d: (dom, (zz << 2) + x_places[d]) for d in range(1, 4)}
    z_peers = {d: (dom, (z_places[d] << 2) + xx) for d in range(1, 8)}

    def inner_peer(offset):
        return inner[offset]

    def outer_peer(dy, dc):
        return outer[dy & 3, dc]

    def x_peer(d):
        return x_peers[d]

    def z_peer(d):
        return z_peers[d]

    def requester(s):
        if s < N_IN:
            return inner_peer(-INNER[s])
        dy, dc = OUTER[s - N_IN]
        return outer_peer(4 - dy, dc)

    barrier = pltpu.get_barrier_semaphore()
    peers = [inner_peer(o) for o in INNER] + [outer_peer(*o) for o in OUTER]
    peers += [z_peer(d) for d in (2, 3, 5, 6)]
    for peer in peers:
        pl.semaphore_signal(barrier, inc=1, device_id=peer, device_id_type=MESH)

    start_copy = pltpu.make_async_copy(start_hbm, start, in_sem.at[0])
    start_copy.start()

    def weights_copy(p):
        return pltpu.make_async_copy(
            weights_hbm.at[pl.ds(6 * p, 6)], weights.at[pl.ds(6 * p, 6)], in_sem.at[1 + p]
        )

    for p in range(3):
        weights_copy(p).start()

    listed = columns[...]
    owner = (listed * 3641) >> 16
    tile = listed - owner * TROWS
    owner_part = owner >> 5
    is_local = owner == dom * N_DEV + dev
    is_outer = owner_part != dom
    off = ((owner & (N_DEV - 1)) - dev) & (N_DEV - 1)
    inner_slot = jnp.where(off <= 4, off - 1, jnp.minimum(35 - off, 8))
    dy = ((owner_part >> 1) - yy) & 3
    outer_slot = 2 * dy + ((owner_part + dom) & 1) - 1
    slot = jnp.where(is_outer, N_IN + outer_slot, jnp.where(is_local, -1, inner_slot))
    order = lax.broadcasted_iota(jnp.int32, (TROWS, 4), 0) * 4 + lax.broadcasted_iota(jnp.int32, (TROWS, 4), 1)
    code = order * 32 + tile
    lanes = lax.broadcasted_iota(jnp.int32, (1, 128), 1)
    is_extra = jnp.zeros((TROWS, 4), jnp.bool_)
    bases, extras, doubled = [], [], []
    for s in range(N_MSG):
        mask = slot == s
        lowest = jnp.min(jnp.min(jnp.where(mask, code, 1 << 20), axis=0, keepdims=True), axis=1, keepdims=True)
        bases.append(lowest & 31)
        if s >= N_IN:
            highest = jnp.max(jnp.max(jnp.where(mask, code, -1), axis=0, keepdims=True), axis=1, keepdims=True)
            is_extra = is_extra | (mask & (code == highest) & (code > lowest))
            doubled.append(highest > lowest)
            extras.append(jnp.where(highest > lowest, highest & 31, 0))
    for s in range(N_MSG):
        row = jnp.where(lanes == 0, bases[s], 0)
        if s >= N_IN:
            o = s - N_IN
            extra = extras[o]
            if o % 2 == 1:
                extra = jnp.where(doubled[o + 1], TROWS + (o + 1) // 2 - 1, extra)
            row = jnp.where(lanes == 1, extra, row)
        msg[s] = row
    src_v[...] = jnp.zeros_like(src_v)
    src_v[pl.ds(0, TROWS), pl.ds(0, 4)] = jnp.where(
        is_outer,
        jnp.where(is_extra, TROWS + N_MSG + dy, TROWS + N_IN + outer_slot),
        jnp.where(is_local, tile, TROWS + inner_slot),
    )
    source_copy = pltpu.make_async_copy(src_v, source, in_sem.at[4])
    source_copy.start()

    pl.semaphore_wait(barrier, len(peers))

    def msg_copy(s):
        return pltpu.make_async_remote_copy(
            src_ref=msg.at[s], dst_ref=got.at[s], send_sem=msg_ss.at[s], recv_sem=msg_rs.at[s],
            device_id=inner_peer(INNER[s]) if s < N_IN else outer_peer(*OUTER[s - N_IN]),
            device_id_type=MESH,
        )

    for s in range(N_MSG):
        msg_copy(s).start()

    start_copy.wait()

    def turn(r, total):
        value = start[r].T
        y[0, 0, r] = value[:HALF]
        y[0, 1, r] = value[HALF:]
        y[1, 0, r] = jnp.zeros((HALF, TILE), jnp.float32)
        y[1, 1, r] = jnp.zeros((HALF, TILE), jnp.float32)
        return total + value * value

    squares = lax.fori_loop(0, TROWS, turn, jnp.zeros((WIDTH, TILE), jnp.float32), unroll=3)
    mul[...] = jnp.ones_like(mul)
    sq[...] = lax.dot_general(
        jnp.ones((8, TILE), jnp.float32), squares, NT,
        precision=lax.Precision.HIGHEST, preferred_element_type=jnp.float32,
    )

    def dom_copy(src, dst, o, send, recv_sem):
        dy, dc = OUTER[o]
        return pltpu.make_async_remote_copy(
            src_ref=src, dst_ref=dst, send_sem=send, recv_sem=recv_sem,
            device_id=outer_peer(dy, dc), device_id_type=MESH,
        )

    def sq_dom(o):
        return dom_copy(sq, sqd.at[o], o, sq_ss.at[o], sq_rs.at[o])

    def sq_x(d):
        return pltpu.make_async_remote_copy(
            src_ref=sqs.at[0], dst_ref=sqx.at[d - 1], send_sem=sq_ss.at[6 + d], recv_sem=sq_rs.at[6 + d],
            device_id=x_peer(d), device_id_type=MESH,
        )

    def sq_z(d):
        return pltpu.make_async_remote_copy(
            src_ref=sqs.at[1], dst_ref=sqz.at[d - 1], send_sem=sq_ss.at[9 + d], recv_sem=sq_rs.at[9 + d],
            device_id=z_peer(d), device_id_type=MESH,
        )

    for o in range(N_OUT):
        sq_dom(o).start()

    ones = jnp.ones((8, TILE), jnp.bfloat16)

    def degrees(r, _):
        total = (weights[r, 0] + weights[r, 1]) + (weights[r, 2] + weights[r, 3])
        hi, lo = split(total.astype(jnp.float32))
        degree = lax.dot_general(ones, hi, NT, preferred_element_type=jnp.float32)
        degree += lax.dot_general(ones, lo, NT, preferred_element_type=jnp.float32)
        scale[r] = lax.rsqrt(degree)
        return 0

    for p in range(3):
        weights_copy(p).wait()
        lax.fori_loop(6 * p, 6 * p + 6, degrees, 0, unroll=6)

    def prepare(r, _):
        for k in range(4):
            hi, lo = split(weights[r, k].astype(jnp.float32).T)
            place = pl.ds((k % 2) * 128, 128)
            wb[r, k // 2, place, pl.ds(0, 128)] = hi
            wb[r, k // 2, place, pl.ds(128, 128)] = lo
        return 0

    def put_scaled(h, r, value):
        z = value * scale[r, pl.ds(0, 1), :]
        zf[h, r] = z
        hi, mid = split(z)
        zb[h, r, pl.ds(0, HALF), :] = hi
        zb[h, r, pl.ds(HALF, HALF), :] = mid

    def slot_copy(h, par, s):
        if s < N_MSG:
            to = requester(s)
        elif s == N_MSG:
            to = outer_peer(0, 1)
        else:
            to = outer_peer(4 - (s - N_MSG), 0)
        return pltpu.make_async_remote_copy(
            src_ref=stage.at[h, s], dst_ref=recv.at[h, par, s],
            send_sem=ss.at[h, s], recv_sem=rs.at[h, par, s],
            device_id=to, device_id_type=MESH,
        )

    def relay_copy(h, par, d):
        return pltpu.make_async_remote_copy(
            src_ref=stage.at[h, N_SLOT + d], dst_ref=relay.at[h, par, d],
            send_sem=relay_ss.at[h, d], recv_sem=relay_rs.at[h, par, d],
            device_id=outer_peer(0, 1), device_id_type=MESH,
        )

    def send_first(h, par):
        for d in range(3):
            stage[h, N_SLOT + d] = zf[h, serve[N_IN + 2 * (d + 1), 0, 1]]
            relay_copy(h, par, d).start()
        for s in (9, 10, 11, 12, 13, 14, 15, 8, 7, 3, 6, 2, 5, 1, 4, 0, 16):
            index = serve[N_IN, 0, 1] if s == N_MSG else serve[s, 0, 0]
            stage[h, s] = zf[h, index]
            slot_copy(h, par, s).start()

    def send_last(h, par):
        for d in range(3):
            relay_copy(h, par, d).wait_recv()
            zf[h, TROWS + d] = relay[h, par, d]
        for d in range(3):
            s = N_MSG + 1 + d
            stage[h, s] = zf[h, serve[N_IN + 2 * (d + 1) - 1, 0, 1]]
            slot_copy(h, par, s).start()

    def operand(h, r, k):
        return jnp.concatenate([zb[h, source[r, k]], zb[h, source[r, k + 1]]], axis=1)

    def near(h):
        def one(r, _):
            part[h, r] = quad(jnp.dot(operand(h, r, 0), wb[r, 0], preferred_element_type=jnp.float32))
            return 0
        lax.fori_loop(0, TROWS, one, 0, unroll=18)

    for h in range(2):
        def first(r, _):
            put_scaled(h, r, y[0, h, r])
            return 0
        lax.fori_loop(0, TROWS, first, 0, unroll=3)
    for s in range(N_MSG):
        msg_copy(s).wait()
    to_smem = pltpu.make_async_copy(got, serve, smem_sem)
    to_smem.start()
    to_smem.wait()
    source_copy.wait()
    for h in range(2):
        send_first(h, 0)
    for h in range(2):
        send_last(h, 0)
    lax.fori_loop(0, TROWS, prepare, 0, unroll=3)
    for h in range(2):
        near(h)

    def outer_dom(o):
        return outer_doms[OUTER[o]]

    def g1(m, o):
        return dom_copy(red.at[m, outer_dom(o)], r1.at[m, o], o, g_ss.at[m, o], g_rs.at[m, o])

    def g2(m, d, src):
        return pltpu.make_async_remote_copy(
            src_ref=r2.at[m, xx], dst_ref=r2.at[m, src], send_sem=g_ss.at[m, 6 + d], recv_sem=g_rs.at[m, 7 + src],
            device_id=x_peer(d), device_id_type=MESH,
        )

    def g3(m, d, src):
        return pltpu.make_async_remote_copy(
            src_ref=r3.at[m, zz], dst_ref=r3.at[m, src], send_sem=g_ss.at[m, 9 + d], recv_sem=g_rs.at[m, 11 + src],
            device_id=z_peer(d), device_id_type=MESH,
        )

    def g4(m, o, src):
        return dom_copy(rg.at[m, dom], rg.at[m, src], o, g_ss.at[m, 17 + o], g_rs.at[m, 19 + src])

    def sum_start(m, block):
        for d in range(N_DOM):
            red[m, d] = block[16 * d:16 * d + 16]
        for o in range(N_OUT):
            g1(m, o).start()

    def sum_x(m):
        for o in range(N_OUT):
            g1(m, o).wait()
        total = red[m, dom]
        for o in range(N_OUT):
            total += r1[m, o]
        r2[m, xx] = total
        for d in range(1, 4):
            g2(m, d, xx).start()

    def sum_z(m):
        for d in range(1, 4):
            g2(m, d, xx).wait_send()
            g2(m, d, x_places[d]).wait_recv()
        r3[m, zz] = (r2[m, 0] + r2[m, 1]) + (r2[m, 2] + r2[m, 3])
        for d in range(1, 8):
            g3(m, d, zz).start()

    def sum_back(m):
        for d in range(1, 8):
            g3(m, d, zz).wait_send()
            g3(m, d, z_places[d]).wait_recv()
        total = r3[m, 0]
        for d in range(1, 8):
            total += r3[m, d]
        rg[m, dom] = total * (1.0 / NROWS)
        for o in range(N_OUT):
            g4(m, o, dom).start()

    def sum_end(m):
        for o in range(N_OUT):
            g4(m, o, dom).wait_send()
            g4(m, o, outer_dom(o)).wait_recv()
        return jnp.concatenate([rg[m, d] for d in range(N_DOM)], axis=0)

    def widen_block(dst, par):
        def one(r, _):
            lane = pl.ds(pl.multiple_of(r * TILE, TILE), TILE)
            for h in range(2):
                hi, mid = split(y[par, h, r])
                dst[pl.ds(HALF * h, HALF), lane] = hi
                dst[pl.ds(WIDTH + HALF * h, HALF), lane] = mid
            return 0
        lax.fori_loop(0, TROWS, one, 0, unroll=3)

    def iteration(it, _):
        s, h = it >> 1, it & 1
        par = s & 1

        @pl.when(it == 2)
        def _():
            for o in range(N_OUT):
                sq_dom(o).wait()
            total = sq[...]
            for o in range(N_OUT):
                total += sqd[o]
            sqs[0] = total
            for d in range(1, 4):
                sq_x(d).start()

        @pl.when(it == 4)
        def _():
            for d in range(1, 4):
                sq_x(d).wait()
            sqs[1] = (sqs[0] + sqx[0]) + (sqx[1] + sqx[2])
            for d in range(1, 8):
                sq_z(d).start()

        @pl.when(it == 8)
        def _():
            for d in range(1, 8):
                sq_z(d).wait()
            total = sqs[1]
            for d in range(7):
                total += sqz[d]
            factor = lax.rsqrt(total[:1] / NROWS + epsilon)
            factor = jnp.broadcast_to(factor, (WIDTH, WIDTH)).T
            mul[0] = factor[:HALF]
            mul[1] = factor[HALF:]

        @pl.when(it == 10)
        def _():
            mul[...] = jnp.ones_like(mul)
            widen_block(fb, 1)
            sum_start(0, quad(lax.dot_general(fb[...], fb[...], NT, preferred_element_type=jnp.float32)))

        @pl.when(it == 11)
        def _():
            sum_x(0)

        for q in range(N_SLOT):
            slot_copy(h, par, q).wait_recv()

        def widen(q, _):
            hi, mid = split(recv[h, par, q])
            zb[h, TROWS + q, pl.ds(0, HALF), :] = hi
            zb[h, TROWS + q, pl.ds(HALF, HALF), :] = mid
            return 0
        lax.fori_loop(0, N_SLOT, widen, 0, unroll=4)

        def far(r, _):
            part[h, r] += quad(jnp.dot(operand(h, r, 2), wb[r, 1], preferred_element_type=jnp.float32))
            return 0
        lax.fori_loop(0, TROWS, far, 0, unroll=18)

        last = s == DEGREE
        a = jnp.where(s == 0, (1 - center) / half_width, jnp.where(last, 1.0, 2 * (1 - center) / half_width)).astype(jnp.float32)
        b = jnp.where(s == 0, -1 / half_width, jnp.where(last, -1.0, -2 / half_width)).astype(jnp.float32)
        c = jnp.where((s == 0) | last, 0.0, -1.0).astype(jnp.float32)

        def update(r, _):
            value = a * y[par, h, r] + b * (part[h, r] * scale[r, pl.ds(0, 1), :]) + c * y[1 - par, h, r]
            value = value * mul[h]
            y[1 - par, h, r] = value
            put_scaled(h, r, value)
            return 0
        lax.fori_loop(0, TROWS, update, 0, unroll=6)

        for q in range(N_SLOT):
            slot_copy(h, par, q).wait_send()
        for d in range(3):
            relay_copy(h, par, d).wait_send()

        @pl.when(s < DEGREE)
        def _():
            send_first(h, 1 - par)
            near(h)
            send_last(h, 1 - par)
        return 0

    lax.fori_loop(0, 2 * (DEGREE + 1), iteration, 0)

    widen_block(ib, 0)
    sum_start(1, quad(lax.dot_general(fb[...], ib[...], NT, preferred_element_type=jnp.float32)))
    sum_z(0)

    def finish(r, _):
        turned[r] = jnp.concatenate([y[1, 0, r], y[1, 1, r]], axis=0).T
        return 0
    lax.fori_loop(0, TROWS, finish, 0, unroll=3)
    out_copy = pltpu.make_async_copy(turned, filtered, out_sem)
    out_copy.start()

    sum_x(1)
    sum_back(0)
    sum_z(1)
    rows = lax.broadcasted_iota(jnp.int32, (WIDTH, WIDTH), 0)
    cols = lax.broadcasted_iota(jnp.int32, (WIDTH, WIDTH), 1)
    mat_a[...] = sum_end(0)
    mat_m[...] = jnp.where(rows == cols, 1.0, 0.0)

    def eliminate(block, _):
        a = mat_a[...]
        m = mat_m[...]
        done = []
        for i in (0, 2, 4, 6):
            a0, a1, m0, m1 = a[i:i + 1], a[i + 1:i + 2], m[i:i + 1], m[i + 1:i + 2]
            p00, p01, p11 = a0[:, i:i + 1], a0[:, i + 1:i + 2], a1[:, i + 1:i + 2]
            q = 1.0 / p00
            low = p01 * q
            schur = p11 - p01 * low
            t = 1.0 / schur
            u1 = t * (a1 - low * a0)
            u0 = q * a0 - low * u1
            n1 = m1 - low * m0
            v1 = t * n1
            v0 = q * m0 - low * v1
            done += [lax.rsqrt(p00) * m0, lax.rsqrt(schur) * n1]
            keep = rows[:, :1] > i + 1
            c0 = jnp.where(keep, a[:, i:i + 1], 0.0)
            c1 = jnp.where(keep, a[:, i + 1:i + 2], 0.0)
            a = a - c0 * u0 - c1 * u1
            m = m - c0 * v0 - c1 * v1
        lin[pl.ds(pl.multiple_of(block * 8, 8), 8), :] = jnp.concatenate(done, axis=0)
        a = pltpu.roll(a, WIDTH - 8, 1)
        mat_a[pl.ds(0, 120), :] = a[8:]
        mat_a[pl.ds(120, 8), :] = a[:8]
        mat_m[pl.ds(0, 120), :] = m[8:]
        mat_m[pl.ds(120, 8), :] = m[:8]
        return 0

    lax.fori_loop(0, 8, eliminate, 0)
    sum_back(1)
    lax.fori_loop(8, 16, eliminate, 0)
    projected = sum_end(1)
    inverse = lin[...]
    left = jnp.dot(inverse, projected, precision=lax.Precision.HIGHEST, preferred_element_type=jnp.float32)
    ritz[...] = lax.dot_general(left, inverse, NT, precision=lax.Precision.HIGHEST, preferred_element_type=jnp.float32)
    out_copy.wait()


def body(start_block, columns, edge_weights):
    f32, bf16 = jnp.float32, jnp.bfloat16
    vmem = pl.BlockSpec(memory_space=pltpu.VMEM)
    hbm = pl.BlockSpec(memory_space=pl.ANY)
    dma = pltpu.SemaphoreType.DMA
    filtered, ritz = pl.pallas_call(
        kernel,
        out_shape=(
            jax.ShapeDtypeStruct((TROWS, TILE, WIDTH), f32),
            jax.ShapeDtypeStruct((WIDTH, WIDTH), f32),
        ),
        in_specs=[vmem, hbm, hbm],
        out_specs=(hbm, vmem),
        scratch_shapes=[
            pltpu.SMEM((24, 128), jnp.int32),
            pltpu.VMEM((24, 128), jnp.int32),
            pltpu.VMEM((N_MSG, 1, 128), jnp.int32),
            pltpu.VMEM((TROWS, TILE, WIDTH), f32),
            pltpu.VMEM((TROWS, 4, TILE, TILE), jnp.int32),
            pltpu.VMEM((TROWS, TILE, WIDTH), f32),
            pltpu.VMEM((TROWS, 2, 256, 256), bf16),
            pltpu.VMEM((TROWS, 8, TILE), f32),
            pltpu.VMEM((2, 2, TROWS, HALF, TILE), f32),
            pltpu.VMEM((2, TROWS + 3, HALF, TILE), f32),
            pltpu.VMEM((2, N_SRC, 2 * HALF, TILE), bf16),
            pltpu.VMEM((2, TROWS, HALF, TILE), f32),
            pltpu.VMEM((2, HALF, TILE), f32),
            pltpu.VMEM((2, N_SLOT + 3, HALF, TILE), f32),
            pltpu.VMEM((2, 2, N_SLOT, HALF, TILE), f32),
            pltpu.VMEM((2, 2, 3, HALF, TILE), f32),
            pltpu.VMEM((N_MSG, 1, 128), jnp.int32),
            pltpu.SMEM((N_MSG, 1, 128), jnp.int32),
            pltpu.VMEM((256, TROWS * TILE), bf16),
            pltpu.VMEM((256, TROWS * TILE), bf16),
            pltpu.VMEM((8, 128), f32),
            pltpu.VMEM((2, 8, 128), f32),
            pltpu.VMEM((7, 8, 128), f32),
            pltpu.VMEM((3, 8, 128), f32),
            pltpu.VMEM((7, 8, 128), f32),
            pltpu.VMEM((2, N_DOM, 16, 128), f32),
            pltpu.VMEM((2, 7, 16, 128), f32),
            pltpu.VMEM((2, 4, 16, 128), f32),
            pltpu.VMEM((2, 8, 16, 128), f32),
            pltpu.VMEM((2, N_DOM, 16, 128), f32),
            pltpu.VMEM((WIDTH, WIDTH), f32),
            pltpu.VMEM((WIDTH, WIDTH), f32),
            pltpu.VMEM((WIDTH, WIDTH), f32),
            dma((5,)), dma, dma((N_MSG,)), dma((N_MSG,)), dma,
            dma((2, N_SLOT)), dma((2, 2, N_SLOT)), dma((2, 3)), dma((2, 2, 3)),
            dma((17,)), dma((17,)), dma((2, 24)), dma((2, 27)),
        ],
        compiler_params=pltpu.CompilerParams(
            collective_id=0, has_side_effects=True, vmem_limit_bytes=56 * 2**20
        ),
        cost_estimate=pl.CostEstimate(flops=8_000_000_000, bytes_accessed=8_000_000, transcendentals=0),
    )(columns, start_block.reshape(TROWS, TILE, WIDTH), edge_weights)
    return filtered.reshape(TROWS * TILE, WIDTH), ritz


def solution(mesh):
    in_specs = (
        P(("dom", "dev"), None),
        P(("dom", "dev"), None),
        P(("dom", "dev"), None, None, None),
    )
    out_specs = (P(("dom", "dev"), None), P())
    return jax.shard_map(body, mesh=mesh, in_specs=in_specs, out_specs=out_specs, check_vma=False)
```

```python
import functools

import jax
import jax.numpy as jnp
from jax import lax
from jax.experimental import pallas as pl
from jax.experimental.pallas import tpu as pltpu
from jax.sharding import PartitionSpec as P

TILE = 128
WIDTH = 128
TROWS = 18
DEGREE = 5
N_DOM = 8
N_DEV = 32
NROWS = 589824
HALF = 64
INNER = (1, 2, 3, 4, -1, -2, -3, -4, 16)
OUTER = ((0, 1), (1, 0), (1, 1), (2, 0), (2, 1), (3, 0), (3, 1))
N_IN = 9
N_OUT = 7
N_MSG = N_IN + N_OUT
N_SLOT = N_MSG + 4
N_SRC = TROWS + N_SLOT
STEPS = 1

epsilon = 1e-06
center = 1.025
half_width = 0.975

MESH = pl.DeviceIdType.MESH
NT = (((1,), (1,)), ((), ()))


def split(x):
    hi = x.astype(jnp.bfloat16)
    mid = (x - hi.astype(jnp.float32)).astype(jnp.bfloat16)
    return hi, mid


def quad(x):
    n = x.shape[0] // 2
    return (x[n:, 128:] + x[n:, :128]) + (x[:n, 128:] + x[:n, :128])


def kernel(
    columns, start_hbm, weights_hbm,
    filtered, ritz,
    source, src_v, msg, start, weights, turned,
    wb, scale, y, zf, zb, part, mul, stage, recv, relay,
    got, serve, fb, ib, sq, sqs, sqd, sqx, sqz, red, r1, r2, r3, rg, mat_a, mat_m, lin,
    in_sem, out_sem, msg_ss, msg_rs, smem_sem, ss, rs, relay_ss, relay_rs,
    sq_ss, sq_rs, g_ss, g_rs,
):
    dom = lax.axis_index("dom")
    dev = lax.axis_index("dev")
    yy, core = dom >> 1, dom & 1
    zz, xx = dev >> 2, dev & 3

    inner = {o: (dom, (dev + o) & (N_DEV - 1)) for o in INNER}
    inner.update({-16: inner[16]})
    outer_doms = {
        (dy, dc): (((yy + dy) & 3) << 1) + ((core + dc) & 1) for dy in range(4) for dc in range(2)
    }
    outer = {key: (value, dev) for key, value in outer_doms.items()}
    x_places = {d: (xx + d) & 3 for d in range(1, 4)}
    z_places = {d: (zz + d) & 7 for d in range(1, 8)}
    x_peers = {d: (dom, (zz << 2) + x_places[d]) for d in range(1, 4)}
    z_peers = {d: (dom, (z_places[d] << 2) + xx) for d in range(1, 8)}

    def inner_peer(offset):
        return inner[offset]

    def outer_peer(dy, dc):
        return outer[dy & 3, dc]

    def x_peer(d):
        return x_peers[d]

    def z_peer(d):
        return z_peers[d]

    def requester(s):
        if s < N_IN:
            return inner_peer(-INNER[s])
        dy, dc = OUTER[s - N_IN]
        return outer_peer(4 - dy, dc)

    barrier = pltpu.get_barrier_semaphore()
    peers = [inner_peer(o) for o in INNER] + [outer_peer(*o) for o in OUTER]
    peers += [z_peer(d) for d in (2, 3, 5, 6)]
    for peer in peers:
        pl.semaphore_signal(barrier, inc=1, device_id=peer, device_id_type=MESH)

    start_copy = pltpu.make_async_copy(start_hbm, start, in_sem.at[0])
    start_copy.start()

    def weights_copy(p):
        return pltpu.make_async_copy(
            weights_hbm.at[pl.ds(6 * p, 6)], weights.at[pl.ds(6 * p, 6)], in_sem.at[1 + p]
        )

    for p in range(3):
        weights_copy(p).start()

    listed = columns[...]
    owner = (listed * 3641) >> 16
    tile = listed - owner * TROWS
    owner_part = owner >> 5
    is_local = owner == dom * N_DEV + dev
    is_outer = owner_part != dom
    off = ((owner & (N_DEV - 1)) - dev) & (N_DEV - 1)
    inner_slot = jnp.where(off <= 4, off - 1, jnp.minimum(35 - off, 8))
    dy = ((owner_part >> 1) - yy) & 3
    outer_slot = 2 * dy + ((owner_part + dom) & 1) - 1
    slot = jnp.where(is_outer, N_IN + outer_slot, jnp.where(is_local, -1, inner_slot))
    order = lax.broadcasted_iota(jnp.int32, (4, TROWS), 0) * TROWS + lax.broadcasted_iota(jnp.int32, (4, TROWS), 1)
    code = order * 32 + tile
    lanes = lax.broadcasted_iota(jnp.int32, (1, 128), 1)
    is_extra = jnp.zeros((4, TROWS), jnp.bool_)
    bases, extras, doubled = [], [], []
    for s in range(N_MSG):
        mask = slot == s
        lowest = jnp.min(jnp.min(jnp.where(mask, code, 1 << 20), axis=0, keepdims=True), axis=1, keepdims=True)
        bases.append(lowest & 31)
        if s >= N_IN:
            highest = jnp.max(jnp.max(jnp.where(mask, code, -1), axis=0, keepdims=True), axis=1, keepdims=True)
            is_extra = is_extra | (mask & (code == highest) & (code > lowest))
            doubled.append(highest > lowest)
            extras.append(jnp.where(highest > lowest, highest & 31, 0))
    for s in range(N_MSG):
        row = jnp.where(lanes == 0, bases[s], 0)
        if s >= N_IN:
            o = s - N_IN
            extra = extras[o]
            if o % 2 == 1:
                extra = jnp.where(doubled[o + 1], TROWS + (o + 1) // 2 - 1, extra)
            row = jnp.where(lanes == 1, extra, row)
        msg[s] = row
    src_v[...] = jnp.zeros_like(src_v)
    src_v[pl.ds(0, 4), pl.ds(0, TROWS)] = jnp.where(
        is_outer,
        jnp.where(is_extra, TROWS + N_MSG + dy, TROWS + N_IN + outer_slot),
        jnp.where(is_local, tile, TROWS + inner_slot),
    )
    source_copy = pltpu.make_async_copy(src_v, source, in_sem.at[4])
    source_copy.start()

    pl.semaphore_wait(barrier, len(peers))

    def msg_copy(s):
        return pltpu.make_async_remote_copy(
            src_ref=msg.at[s], dst_ref=got.at[s], send_sem=msg_ss.at[s], recv_sem=msg_rs.at[s],
            device_id=inner_peer(INNER[s]) if s < N_IN else outer_peer(*OUTER[s - N_IN]),
            device_id_type=MESH,
        )

    for s in range(N_MSG):
        msg_copy(s).start()

    start_copy.wait()

    def turn(r, total):
        value = start[r].T
        y[0, 0, r] = value[:HALF]
        y[0, 1, r] = value[HALF:]
        y[1, 0, r] = jnp.zeros((HALF, TILE), jnp.float32)
        y[1, 1, r] = jnp.zeros((HALF, TILE), jnp.float32)
        return total + value * value

    squares = lax.fori_loop(0, TROWS, turn, jnp.zeros((WIDTH, TILE), jnp.float32), unroll=3)
    mul[...] = jnp.ones_like(mul)
    sq[...] = lax.dot_general(
        jnp.ones((8, TILE), jnp.float32), squares, NT,
        precision=lax.Precision.HIGHEST, preferred_element_type=jnp.float32,
    )

    def dom_copy(src, dst, o, send, recv_sem):
        dy, dc = OUTER[o]
        return pltpu.make_async_remote_copy(
            src_ref=src, dst_ref=dst, send_sem=send, recv_sem=recv_sem,
            device_id=outer_peer(dy, dc), device_id_type=MESH,
        )

    def sq_dom(o):
        return dom_copy(sq, sqd.at[o], o, sq_ss.at[o], sq_rs.at[o])

    def sq_x(d):
        return pltpu.make_async_remote_copy(
            src_ref=sqs.at[0], dst_ref=sqx.at[d - 1], send_sem=sq_ss.at[6 + d], recv_sem=sq_rs.at[6 + d],
            device_id=x_peer(d), device_id_type=MESH,
        )

    def sq_z(d):
        return pltpu.make_async_remote_copy(
            src_ref=sqs.at[1], dst_ref=sqz.at[d - 1], send_sem=sq_ss.at[9 + d], recv_sem=sq_rs.at[9 + d],
            device_id=z_peer(d), device_id_type=MESH,
        )

    for o in range(N_OUT):
        sq_dom(o).start()

    ones = jnp.ones((8, TILE), jnp.bfloat16)

    def degrees(r, _):
        total = (weights[r, 0] + weights[r, 1]) + (weights[r, 2] + weights[r, 3])
        hi, lo = split(total.astype(jnp.float32))
        degree = lax.dot_general(ones, hi, NT, preferred_element_type=jnp.float32)
        degree += lax.dot_general(ones, lo, NT, preferred_element_type=jnp.float32)
        scale[r] = lax.rsqrt(degree)
        return 0

    for p in range(3):
        weights_copy(p).wait()
        lax.fori_loop(6 * p, 6 * p + 6, degrees, 0, unroll=6)

    def prepare(r, _):
        for k in range(4):
            hi, lo = split(weights[r, k].astype(jnp.float32).T)
            place = pl.ds((k % 2) * 128, 128)
            wb[r, k // 2, place, pl.ds(0, 128)] = hi
            wb[r, k // 2, place, pl.ds(128, 128)] = lo
        return 0

    def put_scaled(h, r, value):
        z = value * scale[r, pl.ds(0, 1), :]
        zf[h, r] = z
        hi, mid = split(z)
        zb[h, r, pl.ds(0, HALF), :] = hi
        zb[h, r, pl.ds(HALF, HALF), :] = mid

    def slot_copy(h, par, s):
        if s < N_MSG:
            to = requester(s)
        elif s == N_MSG:
            to = outer_peer(0, 1)
        else:
            to = outer_peer(4 - (s - N_MSG), 0)
        return pltpu.make_async_remote_copy(
            src_ref=stage.at[h, s], dst_ref=recv.at[h, par, s],
            send_sem=ss.at[h, s], recv_sem=rs.at[h, par, s],
            device_id=to, device_id_type=MESH,
        )

    def relay_copy(h, par, d):
        return pltpu.make_async_remote_copy(
            src_ref=stage.at[h, N_SLOT + d], dst_ref=relay.at[h, par, d],
            send_sem=relay_ss.at[h, d], recv_sem=relay_rs.at[h, par, d],
            device_id=outer_peer(0, 1), device_id_type=MESH,
        )

    def send_first(h, par):
        for d in range(3):
            stage[h, N_SLOT + d] = zf[h, serve[N_IN + 2 * (d + 1), 0, 1]]
            relay_copy(h, par, d).start()
        for s in (9, 10, 11, 12, 13, 14, 15, 8, 7, 3, 6, 2, 5, 1, 4, 0, 16):
            index = serve[N_IN, 0, 1] if s == N_MSG else serve[s, 0, 0]
            stage[h, s] = zf[h, index]
            slot_copy(h, par, s).start()

    def send_last(h, par):
        for d in range(3):
            relay_copy(h, par, d).wait_recv()
            zf[h, TROWS + d] = relay[h, par, d]
        for d in range(3):
            s = N_MSG + 1 + d
            stage[h, s] = zf[h, serve[N_IN + 2 * (d + 1) - 1, 0, 1]]
            slot_copy(h, par, s).start()

    def operand(h, r, k):
        return jnp.concatenate([zb[h, source[k, r]], zb[h, source[k + 1, r]]], axis=1)

    def near(h):
        def one(r, _):
            part[h, r] = quad(jnp.dot(operand(h, r, 0), wb[r, 0], preferred_element_type=jnp.float32))
            return 0
        lax.fori_loop(0, TROWS, one, 0, unroll=18)

    for h in range(2):
        def first(r, _):
            put_scaled(h, r, y[0, h, r])
            return 0
        lax.fori_loop(0, TROWS, first, 0, unroll=3)
    for s in range(N_MSG):
        msg_copy(s).wait()
    to_smem = pltpu.make_async_copy(got, serve, smem_sem)
    to_smem.start()
    to_smem.wait()
    source_copy.wait()
    for h in range(2):
        send_first(h, 0)
    for h in range(2):
        send_last(h, 0)
    lax.fori_loop(0, TROWS, prepare, 0, unroll=3)
    for h in range(2):
        near(h)

    def outer_dom(o):
        return outer_doms[OUTER[o]]

    def g1(m, o):
        return dom_copy(red.at[m, outer_dom(o)], r1.at[m, o], o, g_ss.at[m, o], g_rs.at[m, o])

    def g2(m, d, src):
        return pltpu.make_async_remote_copy(
            src_ref=r2.at[m, xx], dst_ref=r2.at[m, src], send_sem=g_ss.at[m, 6 + d], recv_sem=g_rs.at[m, 7 + src],
            device_id=x_peer(d), device_id_type=MESH,
        )

    def g3(m, d, src):
        return pltpu.make_async_remote_copy(
            src_ref=r3.at[m, zz], dst_ref=r3.at[m, src], send_sem=g_ss.at[m, 9 + d], recv_sem=g_rs.at[m, 11 + src],
            device_id=z_peer(d), device_id_type=MESH,
        )

    def g4(m, o, src):
        return dom_copy(rg.at[m, dom], rg.at[m, src], o, g_ss.at[m, 17 + o], g_rs.at[m, 19 + src])

    def sum_start(m, block):
        for d in range(N_DOM):
            red[m, d] = block[16 * d:16 * d + 16]
        for o in range(N_OUT):
            g1(m, o).start()

    def sum_x(m):
        for o in range(N_OUT):
            g1(m, o).wait()
        total = red[m, dom]
        for o in range(N_OUT):
            total += r1[m, o]
        r2[m, xx] = total
        for d in range(1, 4):
            g2(m, d, xx).start()

    def sum_z(m):
        for d in range(1, 4):
            g2(m, d, xx).wait_send()
            g2(m, d, x_places[d]).wait_recv()
        r3[m, zz] = (r2[m, 0] + r2[m, 1]) + (r2[m, 2] + r2[m, 3])
        for d in range(1, 8):
            g3(m, d, zz).start()

    def sum_back(m):
        for d in range(1, 8):
            g3(m, d, zz).wait_send()
            g3(m, d, z_places[d]).wait_recv()
        total = r3[m, 0]
        for d in range(1, 8):
            total += r3[m, d]
        rg[m, dom] = total * (1.0 / NROWS)
        for o in range(N_OUT):
            g4(m, o, dom).start()

    def sum_end(m):
        for o in range(N_OUT):
            g4(m, o, dom).wait_send()
            g4(m, o, outer_dom(o)).wait_recv()
        return jnp.concatenate([rg[m, d] for d in range(N_DOM)], axis=0)

    def widen_block(dst, par):
        def one(r, _):
            lane = pl.ds(pl.multiple_of(r * TILE, TILE), TILE)
            for h in range(2):
                hi, mid = split(y[par, h, r])
                dst[pl.ds(HALF * h, HALF), lane] = hi
                dst[pl.ds(WIDTH + HALF * h, HALF), lane] = mid
            return 0
        lax.fori_loop(0, TROWS, one, 0, unroll=3)

    def iteration(it, _):
        s, h = it >> 1, it & 1
        par = s & 1

        @pl.when(it == 2)
        def _():
            for o in range(N_OUT):
                sq_dom(o).wait()
            total = sq[...]
            for o in range(N_OUT):
                total += sqd[o]
            sqs[0] = total
            for d in range(1, 4):
                sq_x(d).start()

        @pl.when(it == 4)
        def _():
            for d in range(1, 4):
                sq_x(d).wait()
            sqs[1] = (sqs[0] + sqx[0]) + (sqx[1] + sqx[2])
            for d in range(1, 8):
                sq_z(d).start()

        @pl.when(it == 8)
        def _():
            for d in range(1, 8):
                sq_z(d).wait()
            total = sqs[1]
            for d in range(7):
                total += sqz[d]
            factor = lax.rsqrt(total[:1] / NROWS + epsilon)
            factor = jnp.broadcast_to(factor, (WIDTH, WIDTH)).T
            mul[0] = factor[:HALF]
            mul[1] = factor[HALF:]

        @pl.when(it == 10)
        def _():
            mul[...] = jnp.ones_like(mul)
            widen_block(fb, 1)
            sum_start(0, quad(lax.dot_general(fb[...], fb[...], NT, preferred_element_type=jnp.float32)))

        @pl.when(it == 11)
        def _():
            sum_x(0)

        for q in range(N_SLOT):
            slot_copy(h, par, q).wait_recv()

        def widen(q, _):
            hi, mid = split(recv[h, par, q])
            zb[h, TROWS + q, pl.ds(0, HALF), :] = hi
            zb[h, TROWS + q, pl.ds(HALF, HALF), :] = mid
            return 0
        lax.fori_loop(0, N_SLOT, widen, 0, unroll=4)

        def far(r, _):
            part[h, r] += quad(jnp.dot(operand(h, r, 2), wb[r, 1], preferred_element_type=jnp.float32))
            return 0
        lax.fori_loop(0, TROWS, far, 0, unroll=18)

        last = s == DEGREE
        a = jnp.where(s == 0, (1 - center) / half_width, jnp.where(last, 1.0, 2 * (1 - center) / half_width)).astype(jnp.float32)
        b = jnp.where(s == 0, -1 / half_width, jnp.where(last, -1.0, -2 / half_width)).astype(jnp.float32)
        c = jnp.where((s == 0) | last, 0.0, -1.0).astype(jnp.float32)

        def update(r, _):
            value = a * y[par, h, r] + b * (part[h, r] * scale[r, pl.ds(0, 1), :]) + c * y[1 - par, h, r]
            value = value * mul[h]
            y[1 - par, h, r] = value
            put_scaled(h, r, value)
            return 0
        lax.fori_loop(0, TROWS, update, 0, unroll=6)

        for q in range(N_SLOT):
            slot_copy(h, par, q).wait_send()
        for d in range(3):
            relay_copy(h, par, d).wait_send()

        @pl.when(s < DEGREE)
        def _():
            send_first(h, 1 - par)
            near(h)
            send_last(h, 1 - par)
        return 0

    lax.fori_loop(0, 2 * (DEGREE + 1), iteration, 0)

    widen_block(ib, 0)
    sum_start(1, quad(lax.dot_general(fb[...], ib[...], NT, preferred_element_type=jnp.float32)))
    sum_z(0)

    def finish(r, _):
        turned[r] = jnp.concatenate([y[1, 0, r], y[1, 1, r]], axis=0).T
        return 0
    lax.fori_loop(0, TROWS, finish, 0, unroll=3)
    out_copy = pltpu.make_async_copy(turned, filtered, out_sem)
    out_copy.start()

    sum_x(1)
    sum_back(0)
    sum_z(1)
    rows = lax.broadcasted_iota(jnp.int32, (WIDTH, WIDTH), 0)
    cols = lax.broadcasted_iota(jnp.int32, (WIDTH, WIDTH), 1)
    mat_a[...] = sum_end(0)
    mat_m[...] = jnp.where(rows == cols, 1.0, 0.0)

    def eliminate(block, _):
        a = mat_a[...]
        m = mat_m[...]
        done = []
        for i in (0, 2, 4, 6):
            a0, a1, m0, m1 = a[i:i + 1], a[i + 1:i + 2], m[i:i + 1], m[i + 1:i + 2]
            p00, p01, p11 = a0[:, i:i + 1], a0[:, i + 1:i + 2], a1[:, i + 1:i + 2]
            q = 1.0 / p00
            low = p01 * q
            schur = p11 - p01 * low
            t = 1.0 / schur
            u1 = t * (a1 - low * a0)
            u0 = q * a0 - low * u1
            n1 = m1 - low * m0
            v1 = t * n1
            v0 = q * m0 - low * v1
            done += [lax.rsqrt(p00) * m0, lax.rsqrt(schur) * n1]
            keep = rows[:, :1] > i + 1
            c0 = jnp.where(keep, a[:, i:i + 1], 0.0)
            c1 = jnp.where(keep, a[:, i + 1:i + 2], 0.0)
            a = a - c0 * u0 - c1 * u1
            m = m - c0 * v0 - c1 * v1
        lin[pl.ds(pl.multiple_of(block * 8, 8), 8), :] = jnp.concatenate(done, axis=0)
        a = pltpu.roll(a, WIDTH - 8, 1)
        mat_a[pl.ds(0, 120), :] = a[8:]
        mat_a[pl.ds(120, 8), :] = a[:8]
        mat_m[pl.ds(0, 120), :] = m[8:]
        mat_m[pl.ds(120, 8), :] = m[:8]
        return 0

    lax.fori_loop(0, 8, eliminate, 0)
    sum_back(1)
    lax.fori_loop(8, 16, eliminate, 0)
    projected = sum_end(1)
    inverse = lin[...]
    left = jnp.dot(inverse, projected, precision=lax.Precision.HIGHEST, preferred_element_type=jnp.float32)
    ritz[...] = lax.dot_general(left, inverse, NT, precision=lax.Precision.HIGHEST, preferred_element_type=jnp.float32)
    out_copy.wait()


def body(start_block, columns, edge_weights):
    f32, bf16 = jnp.float32, jnp.bfloat16
    vmem = pl.BlockSpec(memory_space=pltpu.VMEM)
    hbm = pl.BlockSpec(memory_space=pl.ANY)
    dma = pltpu.SemaphoreType.DMA
    filtered, ritz = pl.pallas_call(
        kernel,
        out_shape=(
            jax.ShapeDtypeStruct((TROWS, TILE, WIDTH), f32),
            jax.ShapeDtypeStruct((WIDTH, WIDTH), f32),
        ),
        in_specs=[vmem, hbm, hbm],
        out_specs=(hbm, vmem),
        scratch_shapes=[
            pltpu.SMEM((8, 128), jnp.int32),
            pltpu.VMEM((8, 128), jnp.int32),
            pltpu.VMEM((N_MSG, 1, 128), jnp.int32),
            pltpu.VMEM((TROWS, TILE, WIDTH), f32),
            pltpu.VMEM((TROWS, 4, TILE, TILE), jnp.int32),
            pltpu.VMEM((TROWS, TILE, WIDTH), f32),
            pltpu.VMEM((TROWS, 2, 256, 256), bf16),
            pltpu.VMEM((TROWS, 8, TILE), f32),
            pltpu.VMEM((2, 2, TROWS, HALF, TILE), f32),
            pltpu.VMEM((2, TROWS + 3, HALF, TILE), f32),
            pltpu.VMEM((2, N_SRC, 2 * HALF, TILE), bf16),
            pltpu.VMEM((2, TROWS, HALF, TILE), f32),
            pltpu.VMEM((2, HALF, TILE), f32),
            pltpu.VMEM((2, N_SLOT + 3, HALF, TILE), f32),
            pltpu.VMEM((2, 2, N_SLOT, HALF, TILE), f32),
            pltpu.VMEM((2, 2, 3, HALF, TILE), f32),
            pltpu.VMEM((N_MSG, 1, 128), jnp.int32),
            pltpu.SMEM((N_MSG, 1, 128), jnp.int32),
            pltpu.VMEM((256, TROWS * TILE), bf16),
            pltpu.VMEM((256, TROWS * TILE), bf16),
            pltpu.VMEM((8, 128), f32),
            pltpu.VMEM((2, 8, 128), f32),
            pltpu.VMEM((7, 8, 128), f32),
            pltpu.VMEM((3, 8, 128), f32),
            pltpu.VMEM((7, 8, 128), f32),
            pltpu.VMEM((2, N_DOM, 16, 128), f32),
            pltpu.VMEM((2, 7, 16, 128), f32),
            pltpu.VMEM((2, 4, 16, 128), f32),
            pltpu.VMEM((2, 8, 16, 128), f32),
            pltpu.VMEM((2, N_DOM, 16, 128), f32),
            pltpu.VMEM((WIDTH, WIDTH), f32),
            pltpu.VMEM((WIDTH, WIDTH), f32),
            pltpu.VMEM((WIDTH, WIDTH), f32),
            dma((5,)), dma, dma((N_MSG,)), dma((N_MSG,)), dma,
            dma((2, N_SLOT)), dma((2, 2, N_SLOT)), dma((2, 3)), dma((2, 2, 3)),
            dma((17,)), dma((17,)), dma((2, 24)), dma((2, 27)),
        ],
        compiler_params=pltpu.CompilerParams(
            collective_id=0, has_side_effects=True, vmem_limit_bytes=56 * 2**20
        ),
        cost_estimate=pl.CostEstimate(flops=8_000_000_000, bytes_accessed=8_000_000, transcendentals=0),
    )(columns.T, start_block.reshape(TROWS, TILE, WIDTH), edge_weights)
    def write(block, small, out_block, out_small):
        out_block[...] = block[...]

        @pl.when(pl.program_id(0) == 0)
        def _():
            out_small[...] = small[...]

    rows = TROWS * TILE // STEPS
    return tuple(pl.pallas_call(
        write,
        grid=(STEPS,),
        out_shape=(
            jax.ShapeDtypeStruct((TROWS * TILE, WIDTH), f32),
            jax.ShapeDtypeStruct((WIDTH, WIDTH), f32),
        ),
        in_specs=[pl.BlockSpec((rows, WIDTH), lambda i: (i, 0)), pl.BlockSpec((WIDTH, WIDTH), lambda i: (0, 0))],
        out_specs=(pl.BlockSpec((rows, WIDTH), lambda i: (i, 0)), pl.BlockSpec((WIDTH, WIDTH), lambda i: (0, 0))),
    )(filtered.reshape(TROWS * TILE, WIDTH), ritz))


def solution(mesh):
    in_specs = (
        P(("dom", "dev"), None),
        P(("dom", "dev"), None),
        P(("dom", "dev"), None, None, None),
    )
    out_specs = (P(("dom", "dev"), None), P())
    return jax.shard_map(body, mesh=mesh, in_specs=in_specs, out_specs=out_specs, check_vma=False)
```
